512 devices in a mesh: docs: 32 (over y, x), heads: 16 (over z, core).
Axes of the slice: x: 4, y: 8, z: 8, core: 2. Of those that a mesh axis runs over, the one named last changes fastest.
Arguments:
- queries: bfloat16 [65536, 2048], P(('docs', 'heads')), may hold values from -5 to 5
- keys: bfloat16 [65536, 512], P(('docs', 'heads')), may hold values from -5 to 5
- values: bfloat16 [65536, 512], P(('docs', 'heads')), may hold values from -6 to 6
- lengths: int32 [32], replicated, may hold values from 1 to 3072, as said below
Outputs:
- attended: bfloat16 [65536, 2048], P(('docs', 'heads'))
The draws below stay inside these ranges and needn't reach their ends.
Inputs may be any that keep to these rules, and one draw needn't show every extreme that they name: The lengths sum to 65536; the largest is exactly 3072.
All inputs are finite; a program needn't handle non-finite values.
Results may differ from the reference program's by a relative error of at most 0.009.
Values may be sent and summed in bfloat16 or wider, within the bound.
No kernel may reach another device: no remote copies, remote signals or barrier semaphores. Data moves between devices by JAX's collectives and lax.ppermute only.
A program may use at most 64 MiB of HBM per device.

```python
import math
import jax
import jax.numpy as jnp
from jax import lax

QUERY_HEADS = 16
KEY_VALUE_HEADS = 4
HEAD_SIZE = 128
BLOCK = 2048
PACKED_TOKENS = 65536
LONGEST_DOC = 3072
DOCS = 32


def draw_queries(key, part):
    key = jax.random.fold_in(key, 1)
    final_output = jnp.clip(jax.random.normal(key, (PACKED_TOKENS, QUERY_HEADS * HEAD_SIZE), jnp.float32), -5.0, 5.0)
    return final_output.astype(jnp.bfloat16)


def draw_keys(key, part):
    key = jax.random.fold_in(key, 2)
    final_output = jnp.clip(jax.random.normal(key, (PACKED_TOKENS, KEY_VALUE_HEADS * HEAD_SIZE), jnp.float32), -5.0, 5.0)
    return final_output.astype(jnp.bfloat16)


def draw_lengths(key, part):
    key = jax.random.fold_in(key, 7)
    half_block = BLOCK // 2
    head_pad = jax.random.randint(jax.random.fold_in(key, 1), (), 1, half_block).astype(jnp.int32)
    tail_pad = jax.random.randint(jax.random.fold_in(key, 2), (), 1, half_block).astype(jnp.int32)
    middle_count = DOCS - 4
    middle_total = (DOCS - 5) * BLOCK + half_block + tail_pad - head_pad
    base_length = middle_total // middle_count
    leftover = middle_total - base_length * middle_count
    jitter = jax.random.randint(jax.random.fold_in(key, 3), (middle_count,), 0, BLOCK // 4 + 1).astype(jnp.int32)
    middle = base_length + jitter - jnp.roll(jitter, -1) + (jnp.arange(middle_count, dtype=jnp.int32) < leftover).astype(jnp.int32)
    first_doc = jnp.reshape(half_block + head_pad, (1,)).astype(jnp.int32)
    longest = jnp.full((1,), LONGEST_DOC, jnp.int32)
    last_doc = jnp.reshape(BLOCK - tail_pad, (1,)).astype(jnp.int32)
    return jnp.concatenate([first_doc, longest, middle.astype(jnp.int32), longest, last_doc]).astype(jnp.int32)


def block_levels(key, extent, split, least, largest):
    loudness = 1.0
    for dim, shards_of in split:
        heights = jax.random.uniform(jax.random.fold_in(jax.random.fold_in(key, 6), dim), (shards_of,), jnp.float32, least / len(split), largest / len(split))
        loudness = loudness * jnp.repeat(jnp.exp(heights), extent[dim] // shards_of).reshape((-1,) + (1,) * (len(extent) - 1 - dim))
    return loudness


def gaussian(key, extent, scale, reach, shards=(), kind=jnp.bfloat16):
    loudness = block_levels(key, extent, shards, -0.22, 0.18) if shards else 1.0
    result = jax.random.normal(key, extent, jnp.float32) * scale * loudness
    return jnp.minimum(jnp.maximum(result, -reach), reach).astype(kind)


def setup_inputs(seed: int = 0) -> dict:
    key_list = jax.random.split(jax.random.key(seed), 5)
    queries = draw_queries(jax.random.fold_in(key_list[4], 71), 0)
    keys = draw_keys(jax.random.fold_in(key_list[4], 71), 0)
    values = gaussian(key_list[2], (PACKED_TOKENS, KEY_VALUE_HEADS * HEAD_SIZE), 1.0, 6.0, ((0, 512),))
    lengths = draw_lengths(jax.random.fold_in(key_list[4], 71), 0)
    return {"queries": queries, "keys": keys, "values": values, "lengths": lengths}


def documents_of(places, bounds):
    labels = jnp.sum((bounds[None, :] <= places[:, None]).astype(jnp.int32), axis=1)
    return jnp.where(places >= 0, labels, -1).astype(jnp.int32)


def reference(queries, keys, values, lengths):
    total_len = queries.shape[0]
    query_stride = math.gcd(total_len, 512)
    window_span = LONGEST_DOC + query_stride
    group_width = QUERY_HEADS // KEY_VALUE_HEADS
    bounds = jnp.cumsum(lengths).astype(jnp.int32)
    padded_keys = jnp.concatenate([jnp.zeros((LONGEST_DOC, KEY_VALUE_HEADS * HEAD_SIZE), keys.dtype), keys], axis=0)
    padded_values = jnp.concatenate([jnp.zeros((LONGEST_DOC, KEY_VALUE_HEADS * HEAD_SIZE), values.dtype), values], axis=0)

    def one_block(index):
        first_index = (index * query_stride).astype(jnp.int32)
        query_tile_rows = lax.dynamic_slice_in_dim(queries, first_index, query_stride, 0).astype(jnp.float32)
        query_tile_rows = query_tile_rows.reshape(query_stride, KEY_VALUE_HEADS, group_width, HEAD_SIZE)
        key_tile_rows = lax.dynamic_slice_in_dim(padded_keys, first_index, window_span, 0).astype(jnp.float32).reshape(window_span, KEY_VALUE_HEADS, HEAD_SIZE)
        value_tile_rows = lax.dynamic_slice_in_dim(padded_values, first_index, window_span, 0).astype(jnp.float32).reshape(window_span, KEY_VALUE_HEADS, HEAD_SIZE)
        query_place = first_index + jnp.arange(query_stride, dtype=jnp.int32)
        key_place = first_index - LONGEST_DOC + jnp.arange(window_span, dtype=jnp.int32)
        query_doc = documents_of(query_place, bounds)
        key_doc = documents_of(key_place, bounds)
        scores = jnp.einsum("qhgd,khd->hgqk", query_tile_rows, key_tile_rows, precision=lax.Precision.HIGHEST) * (HEAD_SIZE ** -0.5)
        visible = (key_doc[None, :] == query_doc[:, None]) & (key_place[None, :] <= query_place[:, None])
        scores = jnp.where(visible, scores, -1e30)
        row_max = jnp.max(scores, axis=-1, keepdims=True)
        exponent = jnp.where(visible, jnp.exp(scores - row_max), 0.0)
        denominator = jnp.sum(exponent, axis=-1)
        rounded = exponent.astype(jnp.bfloat16).astype(jnp.float32)
        weighted = jnp.einsum("hgqk,khd->hgqd", rounded, value_tile_rows, precision=lax.Precision.HIGHEST)
        final_output = weighted / denominator[..., None]
        return final_output.transpose(2, 0, 1, 3).reshape(query_stride, QUERY_HEADS * HEAD_SIZE).astype(jnp.bfloat16)

    blocks = lax.map(one_block, jnp.arange(total_len // query_stride, dtype=jnp.int32))
    return blocks.reshape(total_len, QUERY_HEADS * HEAD_SIZE)
```

```python
import math

import jax
import jax.numpy as jnp
from jax import lax
from jax.experimental import pallas as pl
from jax.experimental.pallas import tpu as pltpu
from jax.sharding import Mesh, PartitionSpec as P

QUERY_HEADS = 16
KEY_VALUE_HEADS = 4
HEAD_SIZE = 128
GROUP = QUERY_HEADS // KEY_VALUE_HEADS
ROWS = 128
PIECE = 4 * ROWS
WIDTH = GROUP * HEAD_SIZE
REACH = 6
EXPONENT_SCALE = math.log2(math.e) / math.sqrt(HEAD_SIZE)
MASKED = -1e30
ALL = ("docs", "sub", "chip", "core")
TEAM = ("chip", "core")


def columns(x, index, width):
    return x[:, index * width : (index + 1) * width]


def shift(x, by, count):
    pairs = [(i, (i + by * 4) % count) for i in range(count)]
    return lax.ppermute(x, ALL, pairs)


def attend_kernel(info, low_ref, q_ref, *refs):
    pieces = refs[: REACH + 1]
    out_ref = refs[REACH + 1]
    kv, top, total, acc, sems = refs[REACH + 2 :]
    copies = [pltpu.make_async_copy(pieces[n], kv.at[n], sems.at[n]) for n in range(REACH + 1)]
    for copy in copies:
        copy.start()
    for copy in copies:
        copy.wait()
    base = info[0]

    def update(block, piece, masked):
        key_rows = kv[piece, :, :, 0:HEAD_SIZE].reshape(PIECE, HEAD_SIZE)
        value_rows = kv[piece, :, :, HEAD_SIZE : 2 * HEAD_SIZE].reshape(PIECE, HEAD_SIZE)
        if masked:
            key_place = base - piece * PIECE + lax.broadcasted_iota(jnp.int32, (ROWS, PIECE), 1)
            place = base + block * ROWS + lax.broadcasted_iota(jnp.int32, (ROWS, PIECE), 0)
            low = low_ref[pl.ds(block * ROWS, ROWS), :]
            low = jnp.concatenate([low] * (PIECE // 128), axis=1)
            visible = (key_place >= low) & (key_place <= place)
        for head in range(GROUP):
            query = q_ref[block, :, head * HEAD_SIZE : (head + 1) * HEAD_SIZE]
            scores = lax.dot_general(
                query, key_rows, (((1,), (1,)), ((), ())), preferred_element_type=jnp.float32
            )
            if masked:
                scores = jnp.where(visible, scores, MASKED)
            old = top[head]
            new = jnp.maximum(old, jnp.max(scores, axis=1, keepdims=True))
            wide = jnp.concatenate([new] * (PIECE // 128), axis=1)
            expo = jnp.exp2((scores - wide) * EXPONENT_SCALE)
            factor = jnp.exp2((old - new) * EXPONENT_SCALE)
            part = expo[:, 0:128]
            for n in range(1, PIECE // 128):
                part = part + expo[:, n * 128 : (n + 1) * 128]
            total[head] = total[head] * factor + part
            acc[head] = acc[head] * factor + jnp.dot(
                expo.astype(jnp.bfloat16), value_rows, preferred_element_type=jnp.float32
            )
            top[head] = new

    def one_block(block, unused):
        first_low = info[1 + block]
        last_low = info[5 + block]
        top[...] = jnp.full_like(top, MASKED)
        total[...] = jnp.zeros_like(total)
        acc[...] = jnp.zeros_like(acc)

        def one_piece(piece, unused):
            start = base - piece * PIECE
            needed = start + PIECE > first_low
            whole = (piece > 0) & (start >= last_low)

            @pl.when(needed & whole)
            def _():
                update(block, piece, False)

            @pl.when(needed & jnp.logical_not(whole))
            def _():
                update(block, piece, True)

            return unused

        lax.fori_loop(0, REACH + 1, one_piece, 0)
        for head in range(GROUP):
            denominator = jnp.sum(total[head], axis=1, keepdims=True)
            out_ref[block, :, head * HEAD_SIZE : (head + 1) * HEAD_SIZE] = (
                acc[head] / denominator
            ).astype(jnp.bfloat16)
        return unused

    lax.fori_loop(0, PIECE // ROWS, one_block, 0)


def attend(info, low, query_team, pieces):
    vmem = pl.BlockSpec(memory_space=pltpu.VMEM)
    return pl.pallas_call(
        attend_kernel,
        out_shape=jax.ShapeDtypeStruct((4, ROWS, WIDTH), jnp.bfloat16),
        in_specs=[pl.BlockSpec(memory_space=pltpu.SMEM), vmem, vmem]
        + [pl.BlockSpec(memory_space=pl.ANY)] * len(pieces),
        out_specs=vmem,
        scratch_shapes=[
            pltpu.VMEM((REACH + 1, 4, ROWS, 2 * HEAD_SIZE), jnp.bfloat16),
            pltpu.VMEM((GROUP, ROWS, 128), jnp.float32),
            pltpu.VMEM((GROUP, ROWS, 128), jnp.float32),
            pltpu.VMEM((GROUP, ROWS, HEAD_SIZE), jnp.float32),
            pltpu.SemaphoreType.DMA((REACH + 1,)),
        ],
        compiler_params=pltpu.CompilerParams(vmem_limit_bytes=24 * 1024 * 1024),
        cost_estimate=pl.CostEstimate(
            flops=3_000_000_000, bytes_accessed=4_000_000, transcendentals=6_000_000
        ),
        name="attend",
    )(info, low, query_team, *pieces)


def per_device(queries, keys, values, lengths):
    count = lax.axis_size("docs") * 16
    base = (lax.axis_index("docs") * 4 + lax.axis_index("sub")) * PIECE
    bounds = jnp.cumsum(lengths)
    place = base + jnp.arange(PIECE, dtype=jnp.int32)
    low = jnp.max(jnp.where(bounds[None, :] <= place[:, None], bounds[None, :], 0), axis=1)
    info = jnp.concatenate([base[None], low[0::ROWS], low[ROWS - 1 :: ROWS]]).astype(jnp.int32)
    low = jnp.broadcast_to(low[:, None], (PIECE, 128))

    key_value = jnp.stack(
        [
            jnp.concatenate([columns(keys, n, HEAD_SIZE), columns(values, n, HEAD_SIZE)], axis=1)
            for n in range(KEY_VALUE_HEADS)
        ]
    )
    own = lax.all_to_all(key_value, TEAM, 0, 0, tiled=True)
    query_team = jnp.stack([columns(queries, n, WIDTH) for n in range(KEY_VALUE_HEADS)])
    query_team = lax.all_to_all(query_team, TEAM, 0, 0, tiled=True)
    back1, back2, back3, back4 = (shift(own, by, count) for by in (1, 2, 3, 4))
    back5 = shift(back1, 4, count)
    back6 = shift(back2, 4, count)
    outcome = attend(info, low, query_team, (own, back1, back2, back3, back4, back5, back6))
    outcome = lax.all_to_all(outcome, TEAM, 0, 0, tiled=True)
    return jnp.concatenate([outcome[n] for n in range(KEY_VALUE_HEADS)], axis=1)


def solution(mesh):
    docs = mesh.shape["docs"]
    fine = Mesh(mesh.devices.reshape(docs, 4, 2, 2), ALL)
    rows = P(ALL, None)
    return jax.shard_map(
        per_device,
        mesh=fine,
        in_specs=(rows, rows, rows, P()),
        out_specs=rows,
        check_vma=False,
    )
```

```python
import math

import jax
import jax.numpy as jnp
from jax import lax
from jax.experimental import pallas as pl
from jax.experimental.pallas import tpu as pltpu
from jax.sharding import Mesh, PartitionSpec as P

QUERY_HEADS = 16
KEY_VALUE_HEADS = 4
HEAD_SIZE = 128
GROUP = QUERY_HEADS // KEY_VALUE_HEADS
ROWS = 128
PIECE = 4 * ROWS
WIDTH = GROUP * HEAD_SIZE
REACH = 6
EXPONENT_SCALE = math.log2(math.e) / math.sqrt(HEAD_SIZE)
MASKED = -1e30
ALL = ("docs", "hi", "lo")


def permute(x, docs, target):
    pairs = []
    for doc in range(docs):
        for hi in range(4):
            for lo in range(4):
                to_doc, to_hi, to_lo = target(doc, hi, lo)
                pairs.append((doc * 16 + hi * 4 + lo, (to_doc % docs) * 16 + to_hi * 4 + to_lo))
    return lax.ppermute(x, ALL, pairs)


def to_worker(x, turn, docs):
    return permute(x, docs, lambda doc, hi, lo: (doc, (lo + turn) % 4, hi))


def to_owner(x, turn, docs):
    return permute(x, docs, lambda doc, hi, lo: (doc, lo, (hi - turn) % 4))


def chips_on(x, by, docs):
    def target(doc, hi, lo):
        chip = 2 * doc + lo // 2 + by
        return chip // 2, hi, 2 * (chip % 2) + lo % 2

    return permute(x, docs, target)


def other_core(x, docs):
    return permute(x, docs, lambda doc, hi, lo: (doc, hi, lo ^ 1))


def attend_kernel(info, place_ref, low_ref, column_ref, q_ref, *refs):
    pieces = refs[: REACH + 1]
    out_ref = refs[REACH + 1]
    kv, top, total, acc, sems = refs[REACH + 2 :]
    copies = [pltpu.make_async_copy(pieces[n], kv.at[n], sems.at[n]) for n in range(REACH + 1)]
    for copy in copies:
        copy.start()
    top[...] = jnp.full_like(top, MASKED)
    total[...] = jnp.zeros_like(total)
    acc[...] = jnp.zeros_like(acc)
    for copy in copies:
        copy.wait()
    first_low, last_low = info[REACH + 1], info[REACH + 2]

    def update(piece, masked):
        key_rows = kv[piece, :, :, 0:HEAD_SIZE].reshape(PIECE, HEAD_SIZE)
        value_rows = kv[piece, :, :, HEAD_SIZE : 2 * HEAD_SIZE].reshape(PIECE, HEAD_SIZE)

        def scores_of(head):
            query = q_ref[:, :, head * HEAD_SIZE : (head + 1) * HEAD_SIZE].reshape(PIECE, HEAD_SIZE)
            return lax.dot_general(
                query, key_rows, (((1,), (1,)), ((), ())), preferred_element_type=jnp.float32
            )

        if masked:
            key_place = column_ref[0:1, :] + info[piece]
            low = jnp.concatenate([low_ref[...]] * (PIECE // 128), axis=1)
            place = jnp.concatenate([place_ref[...]] * (PIECE // 128), axis=1)
            visible = (key_place >= low) & (key_place <= place)
        ahead = scores_of(0)
        for head in range(GROUP):
            scores = ahead
            if head + 1 < GROUP:
                ahead = scores_of(head + 1)
            if masked:
                scores = jnp.where(visible, scores, MASKED)
            old = top[head]
            new = jnp.maximum(old, jnp.max(scores, axis=1, keepdims=True))
            wide = jnp.concatenate([new] * (PIECE // 128), axis=1)
            expo = jnp.exp2((scores - wide) * EXPONENT_SCALE)
            factor = jnp.exp2((old - new) * EXPONENT_SCALE)
            part = expo[:, 0:128]
            for n in range(1, PIECE // 128):
                part = part + expo[:, n * 128 : (n + 1) * 128]
            total[head] = total[head] * factor + part
            acc[head] = acc[head] * factor + jnp.dot(
                expo.astype(jnp.bfloat16), value_rows, preferred_element_type=jnp.float32
            )
            top[head] = new

    def one_piece(piece, unused):
        start = info[piece]
        needed = start + PIECE > first_low
        whole = (piece > 0) & (start >= last_low)

        @pl.when(needed & whole)
        def _():
            update(piece, False)

        @pl.when(needed & jnp.logical_not(whole))
        def _():
            update(piece, True)

        return unused

    lax.fori_loop(0, REACH + 1, one_piece, 0)
    for head in range(GROUP):
        denominator = jnp.sum(total[head], axis=1, keepdims=True)
        out_ref[:, :, head * HEAD_SIZE : (head + 1) * HEAD_SIZE] = (
            (acc[head] / denominator).astype(jnp.bfloat16).reshape(4, ROWS, HEAD_SIZE)
        )


def attend(info, place, low, column, query_team, pieces):
    vmem = pl.BlockSpec(memory_space=pltpu.VMEM)
    return pl.pallas_call(
        attend_kernel,
        out_shape=jax.ShapeDtypeStruct((4, ROWS, WIDTH), jnp.bfloat16),
        in_specs=[pl.BlockSpec(memory_space=pltpu.SMEM), vmem, vmem, vmem, vmem]
        + [pl.BlockSpec(memory_space=pl.ANY)] * len(pieces),
        out_specs=vmem,
        scratch_shapes=[
            pltpu.VMEM((REACH + 1, 4, ROWS, 2 * HEAD_SIZE), jnp.bfloat16),
            pltpu.VMEM((GROUP, PIECE, 128), jnp.float32),
            pltpu.VMEM((GROUP, PIECE, 128), jnp.float32),
            pltpu.VMEM((GROUP, PIECE, HEAD_SIZE), jnp.float32),
            pltpu.SemaphoreType.DMA((REACH + 1,)),
        ],
        compiler_params=pltpu.CompilerParams(vmem_limit_bytes=40 * 1024 * 1024),
        cost_estimate=pl.CostEstimate(
            flops=3_000_000_000, bytes_accessed=4_000_000, transcendentals=6_000_000
        ),
        name="attend",
    )(info, place, low, column, query_team, *pieces)


def per_device(queries, keys, values, lengths):
    docs = lax.axis_size("docs")
    hi, lo = lax.axis_index("hi"), lax.axis_index("lo")

    def head_of(turn):
        return lax.rem(lo + turn, 4)

    def columns(x, turn, width):
        return lax.dynamic_slice_in_dim(x, head_of(turn) * width, width, 1)

    own = jnp.stack(
        [
            to_worker(
                jnp.concatenate(
                    [columns(keys, turn, HEAD_SIZE), columns(values, turn, HEAD_SIZE)], axis=1
                ),
                turn,
                docs,
            )
            for turn in range(4)
        ]
    )
    query_team = jnp.stack(
        [to_worker(columns(queries, turn, WIDTH), turn, docs) for turn in range(4)]
    )

    back = [chips_on(own, by, docs) for by in (1, 2, 3)]
    near, far = other_core(back[0], docs), other_core(back[1], docs)
    core = lax.rem(lo, 2)
    mixed = other_core(jnp.where(core == 0, own, back[2]), docs)

    base = (lax.axis_index("docs") * 4 + lo) * PIECE
    behind = jnp.stack([0, 2, 4, 6, 1 + 2 * core, 3 + 2 * core, 5 - 4 * core]).astype(jnp.int32)
    quarter = lax.rem(hi - jnp.arange(4, dtype=jnp.int32) + 4, 4)
    column = (quarter[:, None] * ROWS + jnp.arange(ROWS, dtype=jnp.int32)[None, :]).reshape(PIECE)
    place = base + column
    bounds = jnp.cumsum(lengths)
    low = jnp.max(jnp.where(bounds[None, :] <= place[:, None], bounds[None, :], 0), axis=1)
    info = jnp.concatenate(
        [base - behind * PIECE, jnp.min(low)[None], jnp.max(low)[None]]
    ).astype(jnp.int32)
    outcome = attend(
        info,
        jnp.broadcast_to(place[:, None], (PIECE, 128)),
        jnp.broadcast_to(low[:, None], (PIECE, 128)),
        jnp.broadcast_to(column[None, :], (8, PIECE)),
        query_team,
        (own, *back, near, far, mixed),
    )
    outcome = [to_owner(outcome[turn], turn, docs) for turn in range(4)]
    twice = jnp.concatenate(outcome + outcome, axis=1)
    return lax.dynamic_slice_in_dim(twice, lax.rem(4 - lo, 4) * WIDTH, QUERY_HEADS * HEAD_SIZE, 1)


def solution(mesh):
    docs = mesh.shape["docs"]
    fine = Mesh(mesh.devices.reshape(docs, 4, 4), ALL)
    rows = P(ALL, None)
    return jax.shard_map(
        per_device,
        mesh=fine,
        in_specs=(rows, rows, rows, P()),
        out_specs=rows,
        check_vma=False,
    )
```

```python
import functools
import math

import jax
import jax.numpy as jnp
from jax import lax
from jax.experimental import pallas as pl
from jax.experimental.pallas import tpu as pltpu
from jax.sharding import Mesh, PartitionSpec as P

QUERY_HEADS = 16
KEY_VALUE_HEADS = 4
HEAD_SIZE = 128
GROUP = QUERY_HEADS // KEY_VALUE_HEADS
ROWS = 128
PIECE = 4 * ROWS
WIDTH = GROUP * HEAD_SIZE
REACH = 6
EXPONENT_SCALE = math.log2(math.e) / math.sqrt(HEAD_SIZE)
MASKED = -1e30
ALL = ("docs", "sub", "chip", "core")
TEAM = ("chip", "core")


def shift(x, by, docs):
    count = docs * 16
    return lax.ppermute(x, ALL, [(i, (i + by * 4) % count) for i in range(count)])


def rearrange(kernel, shape, *operands):
    return pl.pallas_call(
        kernel,
        out_shape=jax.ShapeDtypeStruct(shape, jnp.bfloat16),
        in_specs=[pl.BlockSpec(memory_space=pltpu.VMEM)] * len(operands),
        out_specs=pl.BlockSpec(memory_space=pltpu.VMEM),
        name=kernel.__name__,
    )(*operands)


def pack_key_value(keys, values, out):
    for n in range(KEY_VALUE_HEADS):
        columns = slice(n * HEAD_SIZE, (n + 1) * HEAD_SIZE)
        out[n, :, 0:HEAD_SIZE] = keys[:, columns]
        out[n, :, HEAD_SIZE : 2 * HEAD_SIZE] = values[:, columns]


def pack_queries(queries, out):
    for n in range(KEY_VALUE_HEADS):
        out[n] = queries[:, n * WIDTH : (n + 1) * WIDTH]


def unpack(outcome, out):
    for n in range(KEY_VALUE_HEADS):
        out[:, n * WIDTH : (n + 1) * WIDTH] = outcome[n]


def attend_kernel(behind, first, last, info, low_ref, q_ref, *refs):
    refs = list(refs)
    pieces = [refs.pop(0) for _ in behind]
    state_in = [] if first else [refs.pop(0) for _ in range(3)]
    out_refs = [refs.pop(0) for _ in range(1 if last else 3)]
    kv, sems = refs[:2]
    top, total, acc = refs[2:] if last else out_refs
    copies = [
        pltpu.make_async_copy(piece, kv.at[n], sems.at[n]) for n, piece in enumerate(pieces)
    ]
    for copy in copies:
        copy.start()
    if first:
        top[...] = jnp.full_like(top, MASKED)
        total[...] = jnp.zeros_like(total)
        acc[...] = jnp.zeros_like(acc)
    else:
        for held, given in zip((top, total, acc), state_in):
            held[...] = given[...]
    for copy in copies:
        copy.wait()
    base, first_low, last_low = info[0], info[1], info[2]

    def update(n, start, masked):
        key_rows = kv[n, :, :, 0:HEAD_SIZE].reshape(PIECE, HEAD_SIZE)
        value_rows = kv[n, :, :, HEAD_SIZE : 2 * HEAD_SIZE].reshape(PIECE, HEAD_SIZE)

        def scores_of(head):
            query = q_ref[:, :, head * HEAD_SIZE : (head + 1) * HEAD_SIZE].reshape(PIECE, HEAD_SIZE)
            return lax.dot_general(
                query, key_rows, (((1,), (1,)), ((), ())), preferred_element_type=jnp.float32
            )

        if masked:
            key_place = start + lax.broadcasted_iota(jnp.int32, (PIECE, PIECE), 1)
            place = base + lax.broadcasted_iota(jnp.int32, (PIECE, PIECE), 0)
            low = jnp.concatenate([low_ref[...]] * (PIECE // 128), axis=1)
            visible = (key_place >= low) & (key_place <= place)
        ahead = scores_of(0)
        for head in range(GROUP):
            scores = ahead
            if head + 1 < GROUP:
                ahead = scores_of(head + 1)
            if masked:
                scores = jnp.where(visible, scores, MASKED)
            old = top[head]
            new = jnp.maximum(old, jnp.max(scores, axis=1, keepdims=True))
            wide = jnp.concatenate([new] * (PIECE // 128), axis=1)
            expo = jnp.exp2((scores - wide) * EXPONENT_SCALE)
            factor = jnp.exp2((old - new) * EXPONENT_SCALE)
            part = expo[:, 0:128]
            for k in range(1, PIECE // 128):
                part = part + expo[:, k * 128 : (k + 1) * 128]
            total[head] = total[head] * factor + part
            acc[head] = acc[head] * factor + jnp.dot(
                expo.astype(jnp.bfloat16), value_rows, preferred_element_type=jnp.float32
            )
            top[head] = new

    def one_piece(n, unused):
        back = n + behind[0]
        start = base - back * PIECE
        needed = start + PIECE > first_low
        whole = (back > 0) & (start >= last_low)

        @pl.when(needed & whole)
        def _():
            update(n, start, False)

        @pl.when(needed & jnp.logical_not(whole))
        def _():
            update(n, start, True)

        return unused

    lax.fori_loop(0, len(behind), one_piece, 0)
    if last:
        for head in range(GROUP):
            denominator = jnp.sum(total[head], axis=1, keepdims=True)
            out_refs[0][:, :, head * HEAD_SIZE : (head + 1) * HEAD_SIZE] = (
                (acc[head] / denominator).astype(jnp.bfloat16).reshape(4, ROWS, HEAD_SIZE)
            )


def attend(info, low, queries, pieces, behind, state, last):
    vmem = pl.BlockSpec(memory_space=pltpu.VMEM)
    part = (GROUP, PIECE, 128)
    held = [jax.ShapeDtypeStruct(part, jnp.float32)] * 3
    done = [jax.ShapeDtypeStruct((4, ROWS, WIDTH), jnp.bfloat16)]
    share = len(behind) / (REACH + 1)
    return pl.pallas_call(
        functools.partial(attend_kernel, behind, not state, last),
        out_shape=done if last else held,
        in_specs=[pl.BlockSpec(memory_space=pltpu.SMEM), vmem, vmem]
        + [pl.BlockSpec(memory_space=pl.ANY)] * len(pieces)
        + [vmem] * len(state),
        out_specs=[vmem] * (1 if last else 3),
        scratch_shapes=[
            pltpu.VMEM((len(behind), 4, ROWS, 2 * HEAD_SIZE), jnp.bfloat16),
            pltpu.SemaphoreType.DMA((len(behind),)),
        ]
        + ([pltpu.VMEM(part, jnp.float32)] * 3 if last else []),
        compiler_params=pltpu.CompilerParams(vmem_limit_bytes=40 * 1024 * 1024),
        cost_estimate=pl.CostEstimate(
            flops=int(3e9 * share), bytes_accessed=4_000_000, transcendentals=int(6e6 * share)
        ),
        name="attend",
    )(info, low, queries, *pieces, *state)


def per_device(queries, keys, values, lengths):
    docs = lax.axis_size("docs")
    base = (lax.axis_index("docs") * 4 + lax.axis_index("sub")) * PIECE
    bounds = jnp.cumsum(lengths)
    place = base + jnp.arange(PIECE, dtype=jnp.int32)
    low = jnp.max(jnp.where(bounds[None, :] <= place[:, None], bounds[None, :], 0), axis=1)
    info = jnp.stack([base, low[0], low[-1]]).astype(jnp.int32)
    low = jnp.broadcast_to(low[:, None], (PIECE, 128))

    key_value = rearrange(pack_key_value, (4, ROWS, 2 * HEAD_SIZE), keys, values)
    own = lax.all_to_all(key_value, TEAM, 0, 0, tiled=True)
    info, low, own = lax.optimization_barrier((info, low, own))
    query_team = rearrange(pack_queries, (4, ROWS, WIDTH), queries)
    query_team = lax.all_to_all(query_team, TEAM, 0, 0, tiled=True)
    back1 = shift(own, 1, docs)
    back3 = shift(own, 3, docs)
    back2 = shift(own, 2, docs)
    back4 = shift(own, 4, docs)
    back5 = shift(back1, 4, docs)
    back6 = shift(back2, 4, docs)
    state = attend(info, low, query_team, (own, back1, back2, back3, back4), range(0, 5), (), False)
    (outcome,) = attend(info, low, query_team, (back5, back6), range(5, 7), state, True)
    outcome = lax.all_to_all(outcome, TEAM, 0, 0, tiled=True)
    return rearrange(unpack, (ROWS, QUERY_HEADS * HEAD_SIZE), outcome)


def solution(mesh):
    docs = mesh.shape["docs"]
    fine = Mesh(mesh.devices.reshape(docs, 4, 2, 2), ALL)
    rows = P(ALL, None)
    return jax.shard_map(
        per_device,
        mesh=fine,
        in_specs=(rows, rows, rows, P()),
        out_specs=rows,
        check_vma=False,
    )
```

```python
import functools
import math

import jax
import jax.numpy as jnp
from jax import lax
from jax.experimental import pallas as pl
from jax.experimental.pallas import tpu as pltpu
from jax.sharding import Mesh, PartitionSpec as P

QUERY_HEADS = 16
KEY_VALUE_HEADS = 4
HEAD_SIZE = 128
GROUP = QUERY_HEADS // KEY_VALUE_HEADS
ROWS = 128
PIECE = 4 * ROWS
WIDTH = GROUP * HEAD_SIZE
REACH = 6
EXPONENT_SCALE = math.log2(math.e) / math.sqrt(HEAD_SIZE)
MASKED = -1e30
ALL = ("docs", "sub", "chip", "core")
TEAM = ("chip", "core")


def columns(x, index, width):
    return x[:, index * width : (index + 1) * width]


def shift(x, by, docs):
    count = docs * 16
    return lax.ppermute(x, ALL, [(i, i + by * 4) for i in range(count - by * 4)])


def turn_back(x, docs):
    pairs = [
        (doc * 16 + sub * 4 + n, doc * 16 + (sub + 3) % 4 * 4 + n)
        for doc in range(docs)
        for sub in range(4)
        for n in range(4)
    ]
    return lax.ppermute(x, ALL, pairs)


def attend_kernel(behind, first, last, info, low_ref, q_ref, *refs):
    refs = list(refs)
    pieces = [refs.pop(0) for _ in behind]
    if not first:
        del refs[:3]
    top, total, acc = [refs.pop(0) for _ in range(3)]
    out_ref = refs.pop(0) if last else None
    kv, sems = refs
    copies = [
        pltpu.make_async_copy(piece, kv.at[n], sems.at[n]) for n, piece in enumerate(pieces)
    ]
    for copy in copies:
        copy.start()
    if first:
        top[...] = jnp.full_like(top, MASKED)
        total[...] = jnp.zeros_like(total)
        acc[...] = jnp.zeros_like(acc)
    for copy in copies:
        copy.wait()
    base, first_low, last_low = info[0], info[1], info[2]

    def update(n, start, masked):
        key_rows = kv[n, :, :, 0:HEAD_SIZE].reshape(PIECE, HEAD_SIZE)
        value_rows = kv[n, :, :, HEAD_SIZE : 2 * HEAD_SIZE].reshape(PIECE, HEAD_SIZE)

        def scores_of(head):
            query = q_ref[:, :, head * HEAD_SIZE : (head + 1) * HEAD_SIZE].reshape(PIECE, HEAD_SIZE)
            return lax.dot_general(
                query, key_rows, (((1,), (1,)), ((), ())), preferred_element_type=jnp.float32
            )

        if masked:
            key_place = start + lax.broadcasted_iota(jnp.int32, (PIECE, PIECE), 1)
            place = base + lax.broadcasted_iota(jnp.int32, (PIECE, PIECE), 0)
            low = jnp.concatenate([low_ref[...]] * (PIECE // 128), axis=1)
            visible = (key_place >= low) & (key_place <= place)
        ahead = scores_of(0)
        for head in range(GROUP):
            scores = ahead
            if head + 1 < GROUP:
                ahead = scores_of(head + 1)
            if masked:
                scores = jnp.where(visible, scores, MASKED)
            old = top[head]
            new = jnp.maximum(old, jnp.max(scores, axis=1, keepdims=True))
            wide = jnp.concatenate([new] * (PIECE // 128), axis=1)
            expo = jnp.exp2((scores - wide) * EXPONENT_SCALE)
            factor = jnp.exp2((old - new) * EXPONENT_SCALE)
            part = expo[:, 0:128]
            for k in range(1, PIECE // 128):
                part = part + expo[:, k * 128 : (k + 1) * 128]
            total[head] = total[head] * factor + part
            acc[head] = acc[head] * factor + jnp.dot(
                expo.astype(jnp.bfloat16), value_rows, preferred_element_type=jnp.float32
            )
            top[head] = new

    def one_piece(n, unused):
        back = behind[0]
        for k in range(1, len(behind)):
            back = jnp.where(n == k, behind[k], back)
        start = base - back * PIECE
        needed = start + PIECE > first_low
        whole = (back > 0) & (start >= last_low)

        @pl.when(needed & whole)
        def _():
            update(n, start, False)

        @pl.when(needed & jnp.logical_not(whole))
        def _():
            update(n, start, True)

        return unused

    lax.fori_loop(0, len(behind), one_piece, 0)
    if last:
        for head in range(GROUP):
            denominator = jnp.sum(total[head], axis=1, keepdims=True)
            out_ref[:, :, head * HEAD_SIZE : (head + 1) * HEAD_SIZE] = (
                (acc[head] / denominator).astype(jnp.bfloat16).reshape(4, ROWS, HEAD_SIZE)
            )


def attend(info, low, queries, pieces, behind, state, last):
    vmem = pl.BlockSpec(memory_space=pltpu.VMEM)
    held = [jax.ShapeDtypeStruct((GROUP, PIECE, 128), jnp.float32)] * 3
    done = [jax.ShapeDtypeStruct((4, ROWS, WIDTH), jnp.bfloat16)] if last else []
    share = len(behind) / (REACH + 1)
    given = 3 + len(pieces)
    return pl.pallas_call(
        functools.partial(attend_kernel, behind, not state, last),
        out_shape=held + done,
        in_specs=[pl.BlockSpec(memory_space=pltpu.SMEM), vmem, vmem]
        + [pl.BlockSpec(memory_space=pl.ANY)] * len(pieces)
        + [vmem] * len(state),
        out_specs=[vmem] * len(held + done),
        scratch_shapes=[
            pltpu.VMEM((len(behind), 4, ROWS, 2 * HEAD_SIZE), jnp.bfloat16),
            pltpu.SemaphoreType.DMA((len(behind),)),
        ],
        input_output_aliases={given + n: n for n in range(len(state))},
        compiler_params=pltpu.CompilerParams(vmem_limit_bytes=40 * 1024 * 1024),
        cost_estimate=pl.CostEstimate(
            flops=int(12e9 * share), bytes_accessed=4_000_000, transcendentals=int(6e6 * share)
        ),
        name="attend",
    )(info, low, queries, *pieces, *state)


def per_device(queries, keys, values, lengths):
    docs = lax.axis_size("docs")
    base = (lax.axis_index("docs") * 4 + lax.axis_index("sub")) * PIECE
    bounds = jnp.cumsum(lengths)
    place = base + jnp.arange(PIECE, dtype=jnp.int32)
    low = jnp.max(jnp.where(bounds[None, :] <= place[:, None], bounds[None, :], 0), axis=1)
    info = jnp.stack([base, low[0], low[-1]]).astype(jnp.int32)
    low = jnp.broadcast_to(low[:, None], (PIECE, 128))

    key_value = jnp.stack(
        [
            jnp.concatenate([columns(keys, n, HEAD_SIZE), columns(values, n, HEAD_SIZE)], axis=1)
            for n in range(KEY_VALUE_HEADS)
        ]
    )
    own = lax.all_to_all(key_value, TEAM, 0, 0, tiled=True)
    info, low, own = lax.optimization_barrier((info, low, own))
    sub = lax.axis_index("sub")
    back1 = shift(own, 1, docs)
    back2 = shift(own, 2, docs)
    back4 = shift(own, 4, docs)
    query_team = jnp.stack([columns(queries, n, WIDTH) for n in range(KEY_VALUE_HEADS)])
    query_team = lax.all_to_all(query_team, TEAM, 0, 0, tiled=True)
    back3 = turn_back(jnp.where(sub == 0, own, back4), docs)
    state = attend(info, low, query_team, (own, back4), (0, 4), (), False)
    back2, *state = lax.optimization_barrier((back2, *state))
    back6 = shift(back2, 4, docs)
    state = attend(info, low, query_team, (back2, back3), (2, 3), state, False)
    back1, *state = lax.optimization_barrier((back1, *state))
    back5 = shift(back1, 4, docs)
    state = attend(info, low, query_team, (back1,), (1,), state, False)
    outcome = attend(info, low, query_team, (back5, back6), (5, 6), state, True)[3]
    outcome = lax.all_to_all(outcome, TEAM, 0, 0, tiled=True)
    return jnp.concatenate([outcome[n] for n in range(KEY_VALUE_HEADS)], axis=1)


def solution(mesh):
    docs = mesh.shape["docs"]
    fine = Mesh(mesh.devices.reshape(docs, 4, 2, 2), ALL)
    rows = P(ALL, None)
    return jax.shard_map(
        per_device,
        mesh=fine,
        in_specs=(rows, rows, rows, P()),
        out_specs=rows,
        check_vma=False,
    )
```

```python
import functools
import math

import jax
import jax.numpy as jnp
from jax import lax
from jax.experimental import pallas as pl
from jax.experimental.pallas import tpu as pltpu
from jax.sharding import Mesh, PartitionSpec as P

QUERY_HEADS = 16
KEY_VALUE_HEADS = 4
HEAD_SIZE = 128
GROUP = QUERY_HEADS // KEY_VALUE_HEADS
ROWS = 128
PIECE = 4 * ROWS
WIDTH = GROUP * HEAD_SIZE
REACH = 6
EXPONENT_SCALE = math.log2(math.e) / math.sqrt(HEAD_SIZE)
MASKED = -1e30
ALL = ("docs", "sub", "chip", "core")
TEAM = ("chip", "core")


def columns(x, index, width):
    return x[:, index * width : (index + 1) * width]


def shift(x, by, docs):
    count = docs * 16
    return lax.ppermute(x, ALL, [(i, i + by * 4) for i in range(count - by * 4)])


def turn_back(x, docs):
    pairs = [
        (doc * 16 + sub * 4 + n, doc * 16 + (sub + 3) % 4 * 4 + n)
        for doc in range(docs)
        for sub in range(4)
        for n in range(4)
    ]
    return lax.ppermute(x, ALL, pairs)


def attend_kernel(behind, first, last, info, low_ref, q_ref, *refs):
    refs = list(refs)
    pieces = [refs.pop(0) for _ in behind]
    if not first:
        del refs[:3]
    top, total, acc = [refs.pop(0) for _ in range(3)]
    out_ref = refs.pop(0) if last else None
    kv, sems = refs
    copies = [
        pltpu.make_async_copy(piece, kv.at[n], sems.at[n]) for n, piece in enumerate(pieces)
    ]
    for copy in copies:
        copy.start()
    if first:
        top[...] = jnp.full_like(top, MASKED)
        total[...] = jnp.zeros_like(total)
        acc[...] = jnp.zeros_like(acc)
    for copy in copies:
        copy.wait()
    base, first_low, last_low = info[0], info[1], info[2]

    def update(n, start, masked):
        key_rows = kv[n, :, :, 0:HEAD_SIZE].reshape(PIECE, HEAD_SIZE)
        value_rows = kv[n, :, :, HEAD_SIZE : 2 * HEAD_SIZE].reshape(PIECE, HEAD_SIZE)

        def scores_of(head):
            query = q_ref[:, :, head * HEAD_SIZE : (head + 1) * HEAD_SIZE].reshape(PIECE, HEAD_SIZE)
            return lax.dot_general(
                query, key_rows, (((1,), (1,)), ((), ())), preferred_element_type=jnp.float32
            )

        if masked:
            key_place = start + lax.broadcasted_iota(jnp.int32, (PIECE, PIECE), 1)
            place = base + lax.broadcasted_iota(jnp.int32, (PIECE, PIECE), 0)
            low = jnp.concatenate([low_ref[...]] * (PIECE // 128), axis=1)
            visible = (key_place >= low) & (key_place <= place)
        ahead = scores_of(0)
        for head in range(GROUP):
            scores = ahead
            if head + 1 < GROUP:
                ahead = scores_of(head + 1)
            if masked:
                scores = jnp.where(visible, scores, MASKED)
            old = top[head]
            new = jnp.maximum(old, jnp.max(scores, axis=1, keepdims=True))
            wide = jnp.concatenate([new] * (PIECE // 128), axis=1)
            expo = jnp.exp2((scores - wide) * EXPONENT_SCALE)
            factor = jnp.exp2((old - new) * EXPONENT_SCALE)
            part = expo[:, 0:128]
            for k in range(1, PIECE // 128):
                part = part + expo[:, k * 128 : (k + 1) * 128]
            total[head] = total[head] * factor + part
            acc[head] = acc[head] * factor + jnp.dot(
                expo.astype(jnp.bfloat16), value_rows, preferred_element_type=jnp.float32
            )
            top[head] = new

    def one_piece(n, unused):
        back = behind[0]
        for k in range(1, len(behind)):
            back = jnp.where(n == k, behind[k], back)
        start = base - back * PIECE
        needed = start + PIECE > first_low
        whole = (back > 0) & (start >= last_low)

        @pl.when(needed & whole)
        def _():
            update(n, start, False)

        @pl.when(needed & jnp.logical_not(whole))
        def _():
            update(n, start, True)

        return unused

    lax.fori_loop(0, len(behind), one_piece, 0)
    if last:
        for head in range(GROUP):
            denominator = jnp.sum(total[head], axis=1, keepdims=True)
            out_ref[:, :, head * HEAD_SIZE : (head + 1) * HEAD_SIZE] = (
                (acc[head] / denominator).astype(jnp.bfloat16).reshape(4, ROWS, HEAD_SIZE)
            )


def attend(info, low, queries, pieces, behind, state, last):
    vmem = pl.BlockSpec(memory_space=pltpu.VMEM)
    held = [jax.ShapeDtypeStruct((GROUP, PIECE, 128), jnp.float32)] * 3
    done = [jax.ShapeDtypeStruct((4, ROWS, WIDTH), jnp.bfloat16)] if last else []
    share = len(behind) / (REACH + 1)
    given = 3 + len(pieces)
    return pl.pallas_call(
        functools.partial(attend_kernel, behind, not state, last),
        out_shape=held + done,
        in_specs=[pl.BlockSpec(memory_space=pltpu.SMEM), vmem, vmem]
        + [pl.BlockSpec(memory_space=pl.ANY)] * len(pieces)
        + [vmem] * len(state),
        out_specs=[vmem] * len(held + done),
        scratch_shapes=[
            pltpu.VMEM((len(behind), 4, ROWS, 2 * HEAD_SIZE), jnp.bfloat16),
            pltpu.SemaphoreType.DMA((len(behind),)),
        ],
        input_output_aliases={given + n: n for n in range(len(state))},
        compiler_params=pltpu.CompilerParams(vmem_limit_bytes=40 * 1024 * 1024),
        cost_estimate=pl.CostEstimate(
            flops=int(12e9 * share), bytes_accessed=4_000_000, transcendentals=int(6e6 * share)
        ),
        name="attend",
    )(info, low, queries, *pieces, *state)


def per_device(queries, keys, values, lengths):
    docs = lax.axis_size("docs")
    query_team = jnp.stack([columns(queries, n, WIDTH) for n in range(KEY_VALUE_HEADS)])
    query_team, keys, values = lax.optimization_barrier((query_team, keys, values))
    query_team = lax.all_to_all(query_team, TEAM, 0, 0, tiled=True)
    key_value = jnp.stack(
        [
            jnp.concatenate([columns(keys, n, HEAD_SIZE), columns(values, n, HEAD_SIZE)], axis=1)
            for n in range(KEY_VALUE_HEADS)
        ]
    )
    own = lax.all_to_all(key_value, TEAM, 0, 0, tiled=True)
    sub = lax.axis_index("sub")
    back1 = shift(own, 1, docs)
    back2 = shift(own, 2, docs)
    back4 = shift(own, 4, docs)
    lengths, back4 = lax.optimization_barrier((lengths, back4))
    base = (lax.axis_index("docs") * 4 + lax.axis_index("sub")) * PIECE
    bounds = jnp.cumsum(lengths)
    place = base + jnp.arange(PIECE, dtype=jnp.int32)
    low = jnp.max(jnp.where(bounds[None, :] <= place[:, None], bounds[None, :], 0), axis=1)
    info = jnp.stack([base, low[0], low[-1]]).astype(jnp.int32)
    low = jnp.broadcast_to(low[:, None], (PIECE, 128))
    back3 = turn_back(jnp.where(sub == 0, own, back4), docs)
    state = attend(info, low, query_team, (own, back4), (0, 4), (), False)
    back1, *state = lax.optimization_barrier((back1, *state))
    back6 = shift(back2, 4, docs)
    back5 = shift(back1, 4, docs)
    state = attend(info, low, query_team, (back1, back2, back3), (1, 2, 3), state, False)
    outcome = attend(info, low, query_team, (back5, back6), (5, 6), state, True)[3]
    outcome = lax.all_to_all(outcome, TEAM, 0, 0, tiled=True)
    return jnp.concatenate([outcome[n] for n in range(KEY_VALUE_HEADS)], axis=1)


def solution(mesh):
    docs = mesh.shape["docs"]
    fine = Mesh(mesh.devices.reshape(docs, 4, 2, 2), ALL)
    rows = P(ALL, None)
    return jax.shard_map(
        per_device,
        mesh=fine,
        in_specs=(rows, rows, rows, P()),
        out_specs=rows,
        check_vma=False,
    )
```

```python
import functools
import math

import jax
import jax.numpy as jnp
from jax import lax
from jax.experimental import pallas as pl
from jax.experimental.pallas import tpu as pltpu
from jax.sharding import Mesh, PartitionSpec as P

QUERY_HEADS = 16
KEY_VALUE_HEADS = 4
HEAD_SIZE = 128
GROUP = QUERY_HEADS // KEY_VALUE_HEADS
ROWS = 128
PIECE = 4 * ROWS
WIDTH = GROUP * HEAD_SIZE
REACH = 6
EXPONENT_SCALE = math.log2(math.e) / math.sqrt(HEAD_SIZE)
MASKED = -1e30
ALL = ("docs", "sub", "chip", "core")
TEAM = ("chip", "core")


def columns(x, index, width):
    return x[:, index * width : (index + 1) * width]


def shift(x, by, docs):
    count = docs * 16
    return lax.ppermute(x, ALL, [(i, i + by * 4) for i in range(count - by * 4)])


def turn_back(x, docs):
    pairs = [
        (doc * 16 + sub * 4 + n, doc * 16 + (sub + 3) % 4 * 4 + n)
        for doc in range(docs)
        for sub in range(4)
        for n in range(4)
    ]
    return lax.ppermute(x, ALL, pairs)


def attend_kernel(behind, first, last, info, low_ref, q_ref, *refs):
    refs = list(refs)
    pieces = [refs.pop(0) for _ in behind]
    if not first:
        del refs[:3]
    top, total, acc = [refs.pop(0) for _ in range(3)]
    out_ref = refs.pop(0) if last else None
    kv, sems = refs
    copies = [
        pltpu.make_async_copy(piece, kv.at[n], sems.at[n]) for n, piece in enumerate(pieces)
    ]
    for copy in copies:
        copy.start()
    if first:
        top[...] = jnp.full_like(top, MASKED)
        total[...] = jnp.zeros_like(total)
        acc[...] = jnp.zeros_like(acc)
    for copy in copies:
        copy.wait()
    base, first_low, last_low = info[0], info[1], info[2]

    def update(n, start, masked):
        key_rows = kv[n, :, :, 0:HEAD_SIZE].reshape(PIECE, HEAD_SIZE)
        value_rows = kv[n, :, :, HEAD_SIZE : 2 * HEAD_SIZE].reshape(PIECE, HEAD_SIZE)

        def scores_of(head):
            query = q_ref[:, :, head * HEAD_SIZE : (head + 1) * HEAD_SIZE].reshape(PIECE, HEAD_SIZE)
            return lax.dot_general(
                query, key_rows, (((1,), (1,)), ((), ())), preferred_element_type=jnp.float32
            )

        if masked:
            key_place = start + lax.broadcasted_iota(jnp.int32, (PIECE, PIECE), 1)
            place = base + lax.broadcasted_iota(jnp.int32, (PIECE, PIECE), 0)
            low = jnp.concatenate([low_ref[...]] * (PIECE // 128), axis=1)
            visible = (key_place >= low) & (key_place <= place)
        ahead = scores_of(0)
        for head in range(GROUP):
            scores = ahead
            if head + 1 < GROUP:
                ahead = scores_of(head + 1)
            if masked:
                scores = jnp.where(visible, scores, MASKED)
            old = top[head]
            new = jnp.maximum(old, jnp.max(scores, axis=1, keepdims=True))
            wide = jnp.concatenate([new] * (PIECE // 128), axis=1)
            expo = jnp.exp2((scores - wide) * EXPONENT_SCALE)
            factor = jnp.exp2((old - new) * EXPONENT_SCALE)
            part = expo[:, 0:128]
            for k in range(1, PIECE // 128):
                part = part + expo[:, k * 128 : (k + 1) * 128]
            total[head] = total[head] * factor + part
            acc[head] = acc[head] * factor + jnp.dot(
                expo.astype(jnp.bfloat16), value_rows, preferred_element_type=jnp.float32
            )
            top[head] = new

    def one_piece(n, unused):
        back = behind[0]
        for k in range(1, len(behind)):
            back = jnp.where(n == k, behind[k], back)
        start = base - back * PIECE
        needed = start + PIECE > first_low
        whole = (back > 0) & (start >= last_low)

        @pl.when(needed & whole)
        def _():
            update(n, start, False)

        @pl.when(needed & jnp.logical_not(whole))
        def _():
            update(n, start, True)

        return unused

    lax.fori_loop(0, len(behind), one_piece, 0)
    if last:
        for head in range(GROUP):
            denominator = jnp.sum(total[head], axis=1, keepdims=True)
            out_ref[:, :, head * HEAD_SIZE : (head + 1) * HEAD_SIZE] = (
                (acc[head] / denominator).astype(jnp.bfloat16).reshape(4, ROWS, HEAD_SIZE)
            )


def attend(info, low, queries, pieces, behind, state, last):
    vmem = pl.BlockSpec(memory_space=pltpu.VMEM)
    held = [jax.ShapeDtypeStruct((GROUP, PIECE, 128), jnp.float32)] * 3
    done = [jax.ShapeDtypeStruct((4, ROWS, WIDTH), jnp.bfloat16)] if last else []
    share = len(behind) / (REACH + 1)
    given = 3 + len(pieces)
    return pl.pallas_call(
        functools.partial(attend_kernel, behind, not state, last),
        out_shape=held + done,
        in_specs=[pl.BlockSpec(memory_space=pltpu.SMEM), vmem, vmem]
        + [pl.BlockSpec(memory_space=pl.ANY)] * len(pieces)
        + [vmem] * len(state),
        out_specs=[vmem] * len(held + done),
        scratch_shapes=[
            pltpu.VMEM((len(behind), 4, ROWS, 2 * HEAD_SIZE), jnp.bfloat16),
            pltpu.SemaphoreType.DMA((len(behind),)),
        ],
        input_output_aliases={given + n: n for n in range(len(state))},
        compiler_params=pltpu.CompilerParams(vmem_limit_bytes=40 * 1024 * 1024),
        cost_estimate=pl.CostEstimate(
            flops=int(12e9 * share), bytes_accessed=4_000_000, transcendentals=int(6e6 * share)
        ),
        name="attend",
    )(info, low, queries, *pieces, *state)


def per_device(queries, keys, values, lengths):
    docs = lax.axis_size("docs")
    query_team = jnp.stack([columns(queries, n, WIDTH) for n in range(KEY_VALUE_HEADS)])
    query_team, keys, values = lax.optimization_barrier((query_team, keys, values))
    query_team = lax.all_to_all(query_team, TEAM, 0, 0, tiled=True)
    key_value = jnp.stack(
        [
            jnp.concatenate([columns(keys, n, HEAD_SIZE), columns(values, n, HEAD_SIZE)], axis=1)
            for n in range(KEY_VALUE_HEADS)
        ]
    )
    own = lax.all_to_all(key_value, TEAM, 0, 0, tiled=True)
    sub = lax.axis_index("sub")
    back1 = shift(own, 1, docs)
    back2 = shift(own, 2, docs)
    back4 = shift(own, 4, docs)
    lengths, back4 = lax.optimization_barrier((lengths, back4))
    base = (lax.axis_index("docs") * 4 + lax.axis_index("sub")) * PIECE
    bounds = jnp.cumsum(lengths)
    place = base + jnp.arange(PIECE, dtype=jnp.int32)
    low = jnp.max(jnp.where(bounds[None, :] <= place[:, None], bounds[None, :], 0), axis=1)
    info = jnp.stack([base, low[0], low[-1]]).astype(jnp.int32)
    low = jnp.broadcast_to(low[:, None], (PIECE, 128))
    back3 = turn_back(jnp.where(sub == 0, own, back4), docs)
    state = attend(info, low, query_team, (own, back4), (0, 4), (), False)
    back1, *state = lax.optimization_barrier((back1, *state))
    back6 = shift(back2, 4, docs)
    back5 = shift(back1, 4, docs)
    state = attend(info, low, query_team, (back1, back2, back3, back6), (1, 2, 3, 6), state, False)
    outcome = attend(info, low, query_team, (back5,), (5,), state, True)[3]
    outcome = lax.all_to_all(outcome, TEAM, 0, 0, tiled=True)
    return jnp.concatenate([outcome[n] for n in range(KEY_VALUE_HEADS)], axis=1)


def solution(mesh):
    docs = mesh.shape["docs"]
    fine = Mesh(mesh.devices.reshape(docs, 4, 2, 2), ALL)
    rows = P(ALL, None)
    return jax.shard_map(
        per_device,
        mesh=fine,
        in_specs=(rows, rows, rows, P()),
        out_specs=rows,
        check_vma=False,
    )
```

```python
import functools
import math

import jax
import jax.numpy as jnp
from jax import lax
from jax.experimental import pallas as pl
from jax.experimental.pallas import tpu as pltpu
from jax.sharding import Mesh, PartitionSpec as P

QUERY_HEADS = 16
KEY_VALUE_HEADS = 4
HEAD_SIZE = 128
GROUP = QUERY_HEADS // KEY_VALUE_HEADS
ROWS = 128
PIECE = 4 * ROWS
WIDTH = GROUP * HEAD_SIZE
REACH = 6
EXPONENT_SCALE = math.log2(math.e) / math.sqrt(HEAD_SIZE)
MASKED = -1e30
ALL = ("docs", "sub", "chip", "core")
TEAM = ("chip", "core")


def columns(x, index, width):
    return x[:, index * width : (index + 1) * width]


def shift(x, by, docs):
    count = docs * 16
    return lax.ppermute(x, ALL, [(i, i + by * 4) for i in range(count - by * 4)])


def turn_back(x, docs):
    pairs = [
        (doc * 16 + sub * 4 + n, doc * 16 + (sub + 3) % 4 * 4 + n)
        for doc in range(docs)
        for sub in range(4)
        for n in range(4)
    ]
    return lax.ppermute(x, ALL, pairs)


def pack_kernel(queries, keys, values, query_out, key_value_out, sems):
    copies = []
    for n in range(KEY_VALUE_HEADS):
        narrow = pl.ds(n * HEAD_SIZE, HEAD_SIZE)
        parts = (
            (keys.at[:, narrow], key_value_out.at[n, :, pl.ds(0, HEAD_SIZE)]),
            (values.at[:, narrow], key_value_out.at[n, :, pl.ds(HEAD_SIZE, HEAD_SIZE)]),
            (queries.at[:, pl.ds(n * WIDTH, WIDTH)], query_out.at[n]),
        )
        for k, (source, target) in enumerate(parts):
            copies.append(pltpu.make_async_copy(source, target, sems.at[n, k]))
    for copy in copies:
        copy.start()
    for copy in copies:
        copy.wait()


def pack(queries, keys, values):
    anywhere = pl.BlockSpec(memory_space=pl.ANY)
    return pl.pallas_call(
        pack_kernel,
        out_shape=[
            jax.ShapeDtypeStruct((KEY_VALUE_HEADS, ROWS, WIDTH), jnp.bfloat16),
            jax.ShapeDtypeStruct((KEY_VALUE_HEADS, ROWS, 2 * HEAD_SIZE), jnp.bfloat16),
        ],
        in_specs=[anywhere] * 3,
        out_specs=[pl.BlockSpec(memory_space=pltpu.VMEM)] * 2,
        scratch_shapes=[pltpu.SemaphoreType.DMA((KEY_VALUE_HEADS, 3))],
        name="pack",
    )(queries, keys, values)


def attend_kernel(behind, first, last, info, low_ref, q_ref, *refs):
    refs = list(refs)
    pieces = [refs.pop(0) for _ in behind]
    if not first:
        del refs[:3]
    top, total, acc = [refs.pop(0) for _ in range(3)]
    out_ref = refs.pop(0) if last else None
    kv, sems = refs
    copies = [
        pltpu.make_async_copy(piece, kv.at[n], sems.at[n]) for n, piece in enumerate(pieces)
    ]
    for copy in copies:
        copy.start()
    if first:
        top[...] = jnp.full_like(top, MASKED)
        total[...] = jnp.zeros_like(total)
        acc[...] = jnp.zeros_like(acc)
    for copy in copies:
        copy.wait()
    base, first_low, last_low = info[0], info[1], info[2]

    def update(n, start, masked):
        key_rows = kv[n, :, :, 0:HEAD_SIZE].reshape(PIECE, HEAD_SIZE)
        value_rows = kv[n, :, :, HEAD_SIZE : 2 * HEAD_SIZE].reshape(PIECE, HEAD_SIZE)

        def scores_of(head):
            query = q_ref[:, :, head * HEAD_SIZE : (head + 1) * HEAD_SIZE].reshape(PIECE, HEAD_SIZE)
            return lax.dot_general(
                query, key_rows, (((1,), (1,)), ((), ())), preferred_element_type=jnp.float32
            )

        if masked:
            key_place = start + lax.broadcasted_iota(jnp.int32, (PIECE, PIECE), 1)
            place = base + lax.broadcasted_iota(jnp.int32, (PIECE, PIECE), 0)
            low = jnp.concatenate([low_ref[...]] * (PIECE // 128), axis=1)
            visible = (key_place >= low) & (key_place <= place)
        ahead = scores_of(0)
        for head in range(GROUP):
            scores = ahead
            if head + 1 < GROUP:
                ahead = scores_of(head + 1)
            if masked:
                scores = jnp.where(visible, scores, MASKED)
            old = top[head]
            new = jnp.maximum(old, jnp.max(scores, axis=1, keepdims=True))
            wide = jnp.concatenate([new] * (PIECE // 128), axis=1)
            expo = jnp.exp2((scores - wide) * EXPONENT_SCALE)
            factor = jnp.exp2((old - new) * EXPONENT_SCALE)
            part = expo[:, 0:128]
            for k in range(1, PIECE // 128):
                part = part + expo[:, k * 128 : (k + 1) * 128]
            total[head] = total[head] * factor + part
            acc[head] = acc[head] * factor + jnp.dot(
                expo.astype(jnp.bfloat16), value_rows, preferred_element_type=jnp.float32
            )
            top[head] = new

    def one_piece(n, unused):
        back = behind[0]
        for k in range(1, len(behind)):
            back = jnp.where(n == k, behind[k], back)
        start = base - back * PIECE
        needed = start + PIECE > first_low
        whole = (back > 0) & (start >= last_low)

        @pl.when(needed & whole)
        def _():
            update(n, start, False)

        @pl.when(needed & jnp.logical_not(whole))
        def _():
            update(n, start, True)

        return unused

    lax.fori_loop(0, len(behind), one_piece, 0)
    if last:
        for head in range(GROUP):
            denominator = jnp.sum(total[head], axis=1, keepdims=True)
            out_ref[:, :, head * HEAD_SIZE : (head + 1) * HEAD_SIZE] = (
                (acc[head] / denominator).astype(jnp.bfloat16).reshape(4, ROWS, HEAD_SIZE)
            )


def attend(info, low, queries, pieces, behind, state, last):
    vmem = pl.BlockSpec(memory_space=pltpu.VMEM)
    held = [jax.ShapeDtypeStruct((GROUP, PIECE, 128), jnp.float32)] * 3
    done = [jax.ShapeDtypeStruct((4, ROWS, WIDTH), jnp.bfloat16)] if last else []
    share = len(behind) / (REACH + 1)
    given = 3 + len(pieces)
    return pl.pallas_call(
        functools.partial(attend_kernel, behind, not state, last),
        out_shape=held + done,
        in_specs=[pl.BlockSpec(memory_space=pltpu.SMEM), vmem, vmem]
        + [pl.BlockSpec(memory_space=pl.ANY)] * len(pieces)
        + [vmem] * len(state),
        out_specs=[vmem] * len(held + done),
        scratch_shapes=[
            pltpu.VMEM((len(behind), 4, ROWS, 2 * HEAD_SIZE), jnp.bfloat16),
            pltpu.SemaphoreType.DMA((len(behind),)),
        ],
        input_output_aliases={given + n: n for n in range(len(state))},
        compiler_params=pltpu.CompilerParams(vmem_limit_bytes=40 * 1024 * 1024),
        cost_estimate=pl.CostEstimate(
            flops=int(12e9 * share), bytes_accessed=4_000_000, transcendentals=int(6e6 * share)
        ),
        name="attend",
    )(info, low, queries, *pieces, *state)


def per_device(queries, keys, values, lengths):
    docs = lax.axis_size("docs")
    query_team, key_value = pack(queries, keys, values)
    query_team = lax.all_to_all(query_team, TEAM, 0, 0, tiled=True)
    own = lax.all_to_all(key_value, TEAM, 0, 0, tiled=True)
    sub = lax.axis_index("sub")
    back1 = shift(own, 1, docs)
    back2 = shift(own, 2, docs)
    back4 = shift(own, 4, docs)
    lengths, back4 = lax.optimization_barrier((lengths, back4))
    base = (lax.axis_index("docs") * 4 + lax.axis_index("sub")) * PIECE
    bounds = jnp.cumsum(lengths)
    place = base + jnp.arange(PIECE, dtype=jnp.int32)
    low = jnp.max(jnp.where(bounds[None, :] <= place[:, None], bounds[None, :], 0), axis=1)
    info = jnp.stack([base, low[0], low[-1]]).astype(jnp.int32)
    low = jnp.broadcast_to(low[:, None], (PIECE, 128))
    back3 = turn_back(jnp.where(sub == 0, own, back4), docs)
    state = attend(info, low, query_team, (own, back4), (0, 4), (), False)
    back1, *state = lax.optimization_barrier((back1, *state))
    back6 = shift(back2, 4, docs)
    back5 = shift(back1, 4, docs)
    state = attend(info, low, query_team, (back1, back2, back3, back6), (1, 2, 3, 6), state, False)
    outcome = attend(info, low, query_team, (back5,), (5,), state, True)[3]
    outcome = lax.all_to_all(outcome, TEAM, 0, 0, tiled=True)
    return jnp.concatenate([outcome[n] for n in range(KEY_VALUE_HEADS)], axis=1)


def solution(mesh):
    docs = mesh.shape["docs"]
    fine = Mesh(mesh.devices.reshape(docs, 4, 2, 2), ALL)
    rows = P(ALL, None)
    return jax.shard_map(
        per_device,
        mesh=fine,
        in_specs=(rows, rows, rows, P()),
        out_specs=rows,
        check_vma=False,
    )
```
